256 devices in a mesh: ctx: 256 (over z, y, x, core).
Axes of the slice: x: 4, y: 4, z: 8, core: 2. Of those that a mesh axis runs over, the one named last changes fastest.
Arguments:
- query_rows: bfloat16 [32768, 128], P('ctx'), may hold values from -6 to 6
- key_rows: bfloat16 [32768, 128], P('ctx'), may hold values from -6 to 6
- value_rows: bfloat16 [32768, 128], P('ctx'), may hold values from -6 to 6
- saved_out: bfloat16 [32768, 128], P('ctx'), may hold values from -6 to 6
- grad_out: bfloat16 [32768, 128], P('ctx')
- saved_lse: bfloat16 [32768], P('ctx'), as said below
Outputs:
- grad_query: bfloat16 [32768, 128], P('ctx')
- grad_key: bfloat16 [32768, 128], P('ctx')
- grad_value: bfloat16 [32768, 128], P('ctx')
The draws below stay inside these ranges and needn't reach their ends.
Inputs may be any that keep to these rules, and one draw needn't show every extreme that they name: `saved_lse`: each entry lies within 0.8 of ln(32768) + 0.5.
All inputs are finite; a program needn't handle non-finite values.
Results may differ from the reference program's by a relative error of at most 0.0084.
Values may be sent and summed in bfloat16 or wider, within the bound.
A program may use at most 192 MiB of HBM per device.

```python
import jax
import jax.numpy as jnp
from jax import lax

HEAD = 128
TOK_DEV = 128
TOKENS = 32768


def draw_grad_out(key, part):
    key = jax.random.fold_in(key, 11)
    values = jax.random.normal(key, (TOKENS, HEAD), jnp.float32)
    return (values * jnp.sqrt(jnp.float32(TOKENS))).astype(jnp.bfloat16)


def draw_saved_lse(key, part):
    key = jax.random.fold_in(key, 23)
    centre = jnp.log(jnp.float32(TOKENS)) + 0.5
    offset = jax.random.uniform(key, (TOKENS,), jnp.float32, -0.5, 0.5)
    return (centre + offset).astype(jnp.bfloat16)


def block_levels(stream_key, shape, cuts, smallest, top_value):
    factor_of, own = 1.0, jax.random.fold_in(stream_key, 6)
    for dim, shards_of in cuts:
        heights = jnp.exp(jax.random.uniform(jax.random.fold_in(own, dim), (shards_of,), jnp.float32, smallest / len(cuts), top_value / len(cuts)))
        factor_of = factor_of * jnp.repeat(heights, shape[dim] // shards_of).reshape([-1 if axis == dim else 1 for axis in range(len(shape))])
    return factor_of


def scatter_about(stream_key, extent, scale, reach, shards=(), kind=jnp.bfloat16):
    result = jax.random.normal(stream_key, extent, jnp.float32) * scale
    if len(shards) > 0:
        result = block_levels(stream_key, extent, shards, -0.22, 0.18) * result
    return jnp.clip(result, min=-reach, max=reach).astype(kind)


def setup_inputs(seed: int = 0) -> dict:
    key_of = jax.random.split(jax.random.key(seed), 7)
    return {
        "query_rows": scatter_about(key_of[0], (TOKENS, HEAD), 1.0, 6.0, ((0, 256),)),
        "key_rows": scatter_about(key_of[1], (TOKENS, HEAD), 1.0, 6.0, ((0, 256),)),
        "value_rows": scatter_about(key_of[2], (TOKENS, HEAD), 1.0, 6.0, ((0, 256),)),
        "saved_out": scatter_about(key_of[3], (TOKENS, HEAD), 1.0, 6.0, ((0, 256),)),
        "grad_out": draw_grad_out(jax.random.fold_in(key_of[6], 71), 0),
        "saved_lse": draw_saved_lse(jax.random.fold_in(key_of[6], 71), 0),
    }


def score_grads(query_part, lse_part, delta_part, grad_part, keys, values, factor):
    logits = jnp.dot(query_part, keys.T, preferred_element_type=jnp.float32) * factor
    weights = jnp.exp(logits - lse_part.astype(jnp.float32)[:, None])
    grad_prob = jnp.dot(grad_part, values.T, preferred_element_type=jnp.float32)
    grad_score = (weights * (grad_prob - delta_part.astype(jnp.float32)[:, None])).astype(jnp.bfloat16)
    return grad_score, weights.astype(jnp.bfloat16)


def reference(query_rows, key_rows, value_rows, saved_out, grad_out, saved_lse):
    factor = HEAD ** -0.5
    row_delta = jnp.sum(grad_out.astype(jnp.float32) * saved_out.astype(jnp.float32), axis=1).astype(jnp.bfloat16)
    block_rows = 8 * TOK_DEV
    starts = jnp.arange(TOKENS // block_rows, dtype=jnp.int32) * block_rows

    def accumulate(carried, begin_row):
        key_sum, value_sum = carried
        query_part = lax.dynamic_slice_in_dim(query_rows, begin_row, block_rows, 0)
        grad_part = lax.dynamic_slice_in_dim(grad_out, begin_row, block_rows, 0)
        lse_part = lax.dynamic_slice_in_dim(saved_lse, begin_row, block_rows, 0)
        delta_part = lax.dynamic_slice_in_dim(row_delta, begin_row, block_rows, 0)
        grad_score, weight_low = score_grads(query_part, lse_part, delta_part, grad_part, key_rows, value_rows, factor)
        query_grad = (factor * jnp.dot(grad_score, key_rows, preferred_element_type=jnp.float32)).astype(jnp.bfloat16)
        key_sum = key_sum + jnp.dot(grad_score.T, query_part, preferred_element_type=jnp.float32)
        value_sum = value_sum + jnp.dot(weight_low.T, grad_part, preferred_element_type=jnp.float32)
        return (key_sum, value_sum), query_grad

    empty_rows = jnp.zeros((TOKENS, HEAD), jnp.float32)
    (key_sum, value_sum), query_grad = lax.scan(accumulate, (empty_rows, empty_rows), starts)
    grad_query = query_grad.reshape(TOKENS, HEAD)
    grad_key = (factor * key_sum).astype(jnp.bfloat16)
    grad_value = value_sum.astype(jnp.bfloat16)
    return grad_query, grad_key, grad_value
```

```python
import math

import jax
import jax.numpy as jnp
from jax import lax
from jax.experimental import pallas as pl
from jax.experimental.pallas import tpu as pltpu
from jax.sharding import PartitionSpec as P

HEAD = 128
TOK = 128
AUX = 16
NX, NY, NZ = 4, 4, 8
SIDE = NX * NY * TOK
TILE = 512
FACTOR = HEAD**-0.5
LOG2E = math.log2(math.e)
F32, BF16 = jnp.float32, jnp.bfloat16
MESH = pl.DeviceIdType.MESH

Z_ORDER = (0, 4, 3, 5, 2, 6, 1, 7)
XY = tuple((dx, dy) for dy in range(NY) for dx in range(NX) if dx or dy)


def dot(a, b):
    return jnp.dot(a, b, preferred_element_type=F32)


def dot_nt(a, b):
    return lax.dot_general(a, b, (((1,), (1,)), ((), ())), preferred_element_type=F32)


def rows(block):
    return pl.ds(block * TOK, TOK)


def kernel(
    q_ref, k_ref, v_ref, so_ref, do_ref, lse_ref, out_ref,
    q_land, d_land, kv, so_buf, lse_buf, q_all, d_all, kt, lse_all, delta_all,
    dq_acc, dk_acc, dv_acc, sib_out, sib_in, z_out, z_in, dq_out, dq_in,
    local_sem, send_sem, q_sem, d_sem, kv_sem, rel_sem, sib_sem, z_sem, dq_sem,
):
    me = lax.axis_index("ctx")
    core, x = lax.rem(me, 2), lax.rem(me // 2, NX)
    y, z = lax.rem(me // (2 * NX), NY), me // (2 * NX * NY)

    def device(core, x, y, z):
        return ((z * NY + y) * NX + x) * 2 + core

    def at_xy(dx, dy):
        return device(core, lax.rem(x + dx, NX), lax.rem(y + dy, NY), z)

    def at_z(dz):
        return device(core, x, y, lax.rem(z + dz, NZ))

    sibling = device(1 - core, x, y, z)

    fetch = [
        pltpu.make_async_copy(src, dst, local_sem.at[i])
        for i, (src, dst) in enumerate((
            (so_ref, so_buf),
            (do_ref, d_land.at[0, pl.ds(0, TOK)]),
            (q_ref, q_land.at[0, pl.ds(0, TOK)]),
            (lse_ref, lse_buf),
            (k_ref, kv.at[0, rows(0)]),
            (v_ref, kv.at[1, rows(0)]),
        ))
    ]
    for copy in fetch:
        copy.start()

    barrier = pltpu.get_barrier_semaphore()
    partners = [sibling]
    partners += [at_xy(dx, dy) for dx, dy in XY]
    partners += [at_z(d) for d in range(1, NZ)]
    for p in partners:
        pl.semaphore_signal(barrier, 1, device_id=(p,), device_id_type=MESH)

    for copy in fetch:
        copy.wait()
    lse_row = jnp.reshape(lse_buf[...].astype(F32), (1, TOK)).astype(BF16)
    q_land[0, pl.ds(TOK, AUX)] = jnp.broadcast_to(lse_row, (AUX, TOK))
    product = d_land[0, pl.ds(0, TOK)].astype(F32) * so_buf[...].astype(F32)
    delta_row = jnp.sum(product.T, axis=0, keepdims=True).astype(BF16)
    d_land[0, pl.ds(TOK, AUX)] = jnp.broadcast_to(delta_row, (AUX, TOK))

    pl.semaphore_wait(barrier, len(partners))

    sends = []

    def send(src, dst, recv_sem, target):
        copy = pltpu.make_async_remote_copy(
            src_ref=src, dst_ref=dst, send_sem=send_sem.at[len(sends)], recv_sem=recv_sem,
            device_id=(target,), device_id_type=MESH,
        )
        copy.start()
        sends.append(copy)

    def arrived(dst, recv_sem):
        pltpu.make_async_remote_copy(
            src_ref=dst, dst_ref=dst, send_sem=send_sem.at[0], recv_sem=recv_sem,
            device_id=(sibling,), device_id_type=MESH,
        ).wait_recv()

    def kv_at(p, other):
        return kv.at[:, rows(2 * p + other)]

    send(kv_at(0, 0), kv_at(0, 1), rel_sem.at[0], sibling)
    near = (1, 3, 2)
    for d in near:
        send(q_land.at[0], q_land.at[d], q_sem.at[d], at_xy(d, 0))
        send(d_land.at[0], d_land.at[d * NX], d_sem.at[d * NX], at_xy(0, d))
    for p, d in enumerate(Z_ORDER):
        if d:
            send(kv_at(0, 0), kv_at(p, 0), kv_sem.at[p], at_z(d))
    for d in near:
        send(q_land.at[0], q_land.at[d * NX], q_sem.at[d * NX], at_xy(0, d))
        send(d_land.at[0], d_land.at[d], d_sem.at[d], at_xy(d, 0))
    for e in near:
        arrived(q_land.at[e], q_sem.at[e])
        for d in near:
            s = d * NX + e
            send(q_land.at[e], q_land.at[s], q_sem.at[s], at_xy(0, d))
        arrived(d_land.at[e * NX], d_sem.at[e * NX])
        for d in near:
            s = e * NX + d
            send(d_land.at[e * NX], d_land.at[s], d_sem.at[s], at_xy(d, 0))

    for s in range(NX * NY):
        if s >= NX:
            arrived(q_land.at[s], q_sem.at[s])
        if s % NX:
            arrived(d_land.at[s], d_sem.at[s])
        q_all[rows(s)] = q_land[s, pl.ds(0, TOK)]
        d_all[rows(s)] = d_land[s, pl.ds(0, TOK)]
        lse_all[:, rows(s)] = q_land[s, pl.ds(TOK, AUX)][0:1].astype(F32) * LOG2E
        delta_all[:, rows(s)] = d_land[s, pl.ds(TOK, AUX)][0:1].astype(F32)

    dq_acc[...] = jnp.zeros_like(dq_acc)
    dk_acc[...] = jnp.zeros_like(dk_acc)
    dv_acc[...] = jnp.zeros_like(dv_acc)

    def tile(ks, qs):
        scores = dot_nt(kv[0, ks], q_all[qs])
        probs = dot_nt(kv[1, ks], d_all[qs])
        weights = jnp.exp2(scores * (FACTOR * LOG2E) - lse_all[:, qs])
        grads = (weights * (probs - delta_all[:, qs])).astype(BF16)
        dv_acc[ks] += dot(weights.astype(BF16), d_all[qs])
        dk_acc[ks] += dot(grads, q_all[qs])
        dq_acc[:, qs] += dot(kt[:, ks], grads)

    def to_sibling(g):
        for p in (2 * g, 2 * g + 1):
            r = rows(2 * p + 1)
            sib_out[p, 0] = dk_acc[r].astype(BF16)
            sib_out[p, 1] = dv_acc[r].astype(BF16)
            send(sib_out.at[p], sib_in.at[p], sib_sem.at[p], sibling)

    def to_owner(g):
        for p in (2 * g, 2 * g + 1):
            r = rows(2 * p)
            arrived(sib_in.at[p], sib_sem.at[p])
            dk = dk_acc[r] + sib_in[p, 0].astype(F32)
            dv = dv_acc[r] + sib_in[p, 1].astype(F32)
            if p == 0:
                dk_acc[r], dv_acc[r] = dk, dv
            else:
                z_out[p, 0], z_out[p, 1] = dk.astype(BF16), dv.astype(BF16)
                send(z_out.at[p], z_in.at[p], z_sem.at[p], at_z(NZ - Z_ORDER[p]))

    for g in range(4):
        for p in (2 * g, 2 * g + 1):
            if p:
                arrived(kv_at(p, 0), kv_sem.at[p])
                send(kv_at(p, 0), kv_at(p, 1), rel_sem.at[p], sibling)
        for p in (2 * g, 2 * g + 1):
            arrived(kv_at(p, 1), rel_sem.at[p])
        ks = pl.ds(g * TILE, TILE)
        kt[:, ks] = kv[0, ks].T

        def step(i, carry):
            tile(ks, pl.ds(pl.multiple_of(i * TILE, TILE), TILE))
            return carry

        lax.fori_loop(0, SIDE // TILE, step, 0)
        to_sibling(g)
        if g:
            to_owner(g - 1)
    to_owner(3)

    for dx, dy in XY:
        s = dy * NX + dx
        dq_out[s] = dq_acc[:, rows(s)].T.astype(BF16)
        send(dq_out.at[s], dq_in.at[s], dq_sem.at[s], at_xy(NX - dx, NY - dy))

    dk, dv = dk_acc[rows(0)], dv_acc[rows(0)]
    for p in range(1, NZ):
        arrived(z_in.at[p], z_sem.at[p])
        dk += z_in[p, 0].astype(F32)
        dv += z_in[p, 1].astype(F32)
    out_ref[1] = (dk * FACTOR).astype(BF16)
    out_ref[2] = dv.astype(BF16)
    dq = dq_acc[:, rows(0)].T
    for s in range(1, NX * NY):
        arrived(dq_in.at[s], dq_sem.at[s])
        dq += dq_in[s].astype(F32)
    out_ref[0] = (dq * FACTOR).astype(BF16)
    for copy in sends:
        copy.wait_send()


def on_device(*args):
    vmem, dma = pltpu.VMEM, pltpu.SemaphoreType.DMA
    blocks = NX * NY
    out = pl.pallas_call(
        kernel,
        out_shape=jax.ShapeDtypeStruct((3, TOK, HEAD), BF16),
        in_specs=[pl.BlockSpec(memory_space=pltpu.HBM)] * 6,
        out_specs=pl.BlockSpec(memory_space=pltpu.VMEM),
        scratch_shapes=[
            vmem((blocks, TOK + AUX, HEAD), BF16),
            vmem((blocks, TOK + AUX, HEAD), BF16),
            vmem((2, SIDE, HEAD), BF16),
            vmem((TOK, HEAD), BF16),
            vmem((TOK,), BF16),
            vmem((SIDE, HEAD), BF16),
            vmem((SIDE, HEAD), BF16),
            vmem((HEAD, SIDE), BF16),
            vmem((1, SIDE), F32),
            vmem((1, SIDE), F32),
            vmem((HEAD, SIDE), F32),
            vmem((SIDE, HEAD), F32),
            vmem((SIDE, HEAD), F32),
            vmem((NZ, 2, TOK, HEAD), BF16),
            vmem((NZ, 2, TOK, HEAD), BF16),
            vmem((NZ, 2, TOK, HEAD), BF16),
            vmem((NZ, 2, TOK, HEAD), BF16),
            vmem((blocks, TOK, HEAD), BF16),
            vmem((blocks, TOK, HEAD), BF16),
            dma((6,)),
            dma((76,)),
            dma((blocks,)),
            dma((blocks,)),
            dma((NZ,)),
            dma((NZ,)),
            dma((NZ,)),
            dma((NZ,)),
            dma((blocks,)),
        ],
        compiler_params=pltpu.CompilerParams(
            collective_id=0, has_side_effects=True, vmem_limit_bytes=62 << 20
        ),
        name="attention_backward",
    )(*args)
    return out[0], out[1], out[2]


def solution(mesh):
    tokens = P("ctx", None)
    return jax.shard_map(
        on_device,
        mesh=mesh,
        in_specs=(tokens,) * 5 + (P("ctx"),),
        out_specs=(tokens,) * 3,
        check_vma=False,
    )
```

```python
import math

import jax
import jax.numpy as jnp
from jax import lax
from jax.experimental import pallas as pl
from jax.experimental.pallas import tpu as pltpu
from jax.sharding import PartitionSpec as P

HEAD = 128
TOK = 128
AUX = 16
NX, NY, NZ = 4, 4, 8
SIDE = NX * NY * TOK
TILE = 512
FACTOR = HEAD**-0.5
LOG2E = math.log2(math.e)
F32, BF16 = jnp.float32, jnp.bfloat16
MESH = pl.DeviceIdType.MESH

Z_ORDER = (0, 1, 7, 2, 6, 3, 5, 4)
AT = {d: p for p, d in enumerate(Z_ORDER)}
A, B, C, D = range(4)
NEAR = (1, 3, 2)


def dot(a, b):
    return jnp.dot(a, b, preferred_element_type=F32)


def dot_nt(a, b):
    return lax.dot_general(a, b, (((1,), (1,)), ((), ())), preferred_element_type=F32)


def rows(block):
    return pl.ds(block * TOK, TOK)


def kernel(
    q_ref, k_ref, v_ref, so_ref, do_ref, lse_ref, out_ref,
    q_land, d_land, kv, so_buf, lse_buf, q_all, d_all, kt, lse_all, delta_all,
    dq_acc, dk_acc, dv_acc, sib_out, sib_in, z_out, z_in, dq_out, dq_in,
    local_sem, send_sem, q_sem, d_sem, kv_sem, rel_sem, sib_sem, z_sem, dq_sem,
):
    me = lax.axis_index("ctx")
    core, x = lax.rem(me, 2), lax.rem(me // 2, NX)
    y, z = lax.rem(me // (2 * NX), NY), me // (2 * NX * NY)

    def device(core, x, y, z):
        return ((z * NY + y) * NX + x) * 2 + core

    def at_xy(dx, dy):
        return device(core, lax.rem(x + dx, NX), lax.rem(y + dy, NY), z)

    def at_z(dz):
        return device(core, x, y, lax.rem(z + dz, NZ))

    sibling = device(1 - core, x, y, z)

    barrier = pltpu.get_barrier_semaphore()
    partners = [sibling]
    partners += [at_xy(d, 0) for d in NEAR] + [at_xy(0, d) for d in NEAR]
    partners += [at_z(d) for d in (1, 7, 2, 6)]
    for p in partners:
        pl.semaphore_signal(barrier, 1, device_id=(p,), device_id_type=MESH)

    fetch = [
        pltpu.make_async_copy(src, dst, local_sem.at[i])
        for i, (src, dst) in enumerate((
            (so_ref, so_buf),
            (do_ref, d_land.at[0, pl.ds(0, TOK)]),
            (q_ref, q_land.at[0, pl.ds(0, TOK)]),
            (lse_ref, lse_buf),
            (k_ref, kv.at[0, rows(0)]),
            (v_ref, kv.at[1, rows(0)]),
        ))
    ]
    for copy in fetch:
        copy.start()
    for copy in fetch:
        copy.wait()
    lse_row = jnp.reshape(lse_buf[...].astype(F32), (1, TOK)).astype(BF16)
    q_land[0, pl.ds(TOK, AUX)] = jnp.broadcast_to(lse_row, (AUX, TOK))
    product = d_land[0, pl.ds(0, TOK)].astype(F32) * so_buf[...].astype(F32)
    delta_row = jnp.sum(product.T, axis=0, keepdims=True).astype(BF16)
    d_land[0, pl.ds(TOK, AUX)] = jnp.broadcast_to(delta_row, (AUX, TOK))
    dq_acc[...] = jnp.zeros_like(dq_acc)
    dk_acc[...] = jnp.zeros_like(dk_acc)
    dv_acc[...] = jnp.zeros_like(dv_acc)
    pl.semaphore_wait(barrier, len(partners))

    def send(src, dst, kind, recv_sem, target):
        pltpu.make_async_remote_copy(
            src_ref=src, dst_ref=dst, send_sem=send_sem.at[kind], recv_sem=recv_sem,
            device_id=(target,), device_id_type=MESH,
        ).start()

    def of(ref, kind, recv_sem):
        return pltpu.make_async_remote_copy(
            src_ref=ref, dst_ref=ref, send_sem=send_sem.at[kind], recv_sem=recv_sem,
            device_id=(sibling,), device_id_type=MESH,
        )

    def arrived(dst, recv_sem):
        of(dst, 0, recv_sem).wait_recv()

    def kv_at(p, other):
        return kv.at[:, rows(2 * p + other)]

    def half(h, p):
        return kv.at[h, rows(2 * p)]

    def send_kv(src, d, dz):
        send(src, kv_at(AT[d], 0), 2, kv_sem.at[AT[d]], at_z(dz))

    def to_other_core(d):
        p = AT[d]
        send(kv_at(p, 0), kv_at(p, 1), 2, rel_sem.at[p], sibling)

    def send_q(src, dx, dy, sem, hx, hy):
        send(q_land.at[src], q_land.at[dy * NX + dx], 0, q_sem.at[sem], at_xy(hx, hy))

    def send_d(src, dx, dy, sem, hx, hy):
        send(d_land.at[src], d_land.at[dy * NX + dx], 1, d_sem.at[sem], at_xy(hx, hy))

    to_other_core(0)
    for d in NEAR:
        send_q(0, d, 0, d, d, 0)
        send_d(0, 0, d, 3 + d, 0, d)
    for d in (2, 6, 1, 7):
        send_kv(kv_at(0, 0), d, d)
    for d in NEAR:
        send_d(0, d, 0, d, d, 0)
        send_q(0, 0, d, 3 + d, 0, d)
    for e in NEAR:
        arrived(q_land.at[e], q_sem.at[e])
        for d in NEAR:
            send_q(e, e, d, 6 + d, 0, d)
        arrived(d_land.at[e * NX], d_sem.at[3 + e])
        for d in NEAR:
            send_d(e * NX, d, e, 6 + e, d, 0)
    for d, far, hop, mid, h in ((2, 3, 1, 2, 0), (6, 5, 7, 6, 1)):
        arrived(kv_at(AT[d], 0), kv_sem.at[AT[d]])
        send_kv(kv_at(AT[d], 0), far, hop)
        send(half(h, AT[d]), half(h, AT[4]), 2, kv_sem.at[AT[4] if h == 0 else 0], at_z(mid))
        to_other_core(d)
    for d in (1, 7):
        arrived(kv_at(AT[d], 0), kv_sem.at[AT[d]])
        to_other_core(d)

    def land(dy):
        for e in NEAR:
            if dy == 0:
                arrived(d_land.at[e], d_sem.at[e])
        if dy:
            arrived(q_land.at[dy * NX], q_sem.at[3 + dy])
            arrived(q_land.at[pl.ds(dy * NX + 1, 3)], q_sem.at[6 + dy])
            arrived(d_land.at[pl.ds(dy * NX + 1, 3)], d_sem.at[6 + dy])
        for s in range(dy * NX, dy * NX + NX):
            q_all[rows(s)] = q_land[s, pl.ds(0, TOK)]
            d_all[rows(s)] = d_land[s, pl.ds(0, TOK)]
            lse_all[:, rows(s)] = q_land[s, pl.ds(TOK, AUX)][0:1].astype(F32) * LOG2E
            delta_all[:, rows(s)] = d_land[s, pl.ds(TOK, AUX)][0:1].astype(F32)

    def keys_ready(g):
        for p in (2 * g, 2 * g + 1):
            arrived(kv_at(p, 1), rel_sem.at[p])
        ks = pl.ds(g * TILE, TILE)
        kt[:, ks] = kv[0, ks].T

    def tile(g, dy):
        start = g * TILE if isinstance(g, int) else pl.multiple_of(g * TILE, TILE)
        ks = pl.ds(start, TILE)
        start = dy * TILE if isinstance(dy, int) else pl.multiple_of(dy * TILE, TILE)
        qs = pl.ds(start, TILE)
        scores = dot_nt(kv[0, ks], q_all[qs])
        probs = dot_nt(kv[1, ks], d_all[qs])
        weights = jnp.exp2(scores * (FACTOR * LOG2E) - lse_all[:, qs])
        grads = (weights * (probs - delta_all[:, qs])).astype(BF16)
        dv_acc[ks] += dot(weights.astype(BF16), d_all[qs])
        dk_acc[ks] += dot(grads, q_all[qs])
        dq_acc[:, qs] += dot(kt[:, ks], grads)

    def over_keys(n, dy):
        lax.fori_loop(0, n, lambda g, c: (tile(g, dy), c)[1], 0)

    def over_queries(g):
        lax.fori_loop(0, NY, lambda i, c: (tile(g, i), c)[1], 0)

    def to_sibling(g):
        for p in (2 * g, 2 * g + 1):
            r = rows(2 * p + 1)
            sib_out[p, 0] = dk_acc[r].astype(BF16)
            sib_out[p, 1] = dv_acc[r].astype(BF16)
            send(sib_out.at[p], sib_in.at[p], 3, sib_sem.at[p], sibling)

    def to_owner(g):
        for p in (2 * g, 2 * g + 1):
            r = rows(2 * p)
            arrived(sib_in.at[p], sib_sem.at[p])
            dk = dk_acc[r] + sib_in[p, 0].astype(F32)
            dv = dv_acc[r] + sib_in[p, 1].astype(F32)
            if p == 0:
                dk_acc[r], dv_acc[r] = dk, dv
            else:
                z_out[p, 0], z_out[p, 1] = dk.astype(BF16), dv.astype(BF16)
                send(z_out.at[p], z_in.at[p], 4, z_sem.at[p], at_z(NZ - Z_ORDER[p]))

    def queries_done(dy):
        for dx in range(NX):
            s = dy * NX + dx
            if s:
                dq_out[s] = dq_acc[:, rows(s)].T.astype(BF16)
                send(dq_out.at[s], dq_in.at[s], 5, dq_sem.at[s], at_xy((NX - dx) % NX, (NY - dy) % NY))

    land(0)
    keys_ready(A)
    keys_ready(B)
    over_keys(2, 0)
    land(1)
    over_keys(2, 1)
    land(3)
    over_keys(2, 3)
    for d in (5, 3):
        arrived(kv_at(AT[d], 0), kv_sem.at[AT[d]])
        to_other_core(d)
    arrived(half(0, AT[4]), kv_sem.at[AT[4]])
    arrived(half(1, AT[4]), kv_sem.at[0])
    to_other_core(4)
    land(2)
    tile(B, 2)
    to_sibling(B)
    keys_ready(D)
    over_queries(D)
    to_sibling(D)
    to_owner(B)
    keys_ready(C)
    tile(C, 0)
    to_owner(D)
    queries_done(0)
    tile(C, 1)
    queries_done(1)
    tile(C, 3)
    queries_done(3)
    tile(C, 2)
    to_sibling(C)
    tile(A, 2)
    to_sibling(A)
    queries_done(2)
    to_owner(C)
    to_owner(A)
    dq = dq_acc[:, rows(0)].T
    for dy in (0, 1, 3, 2):
        for s in range(dy * NX, dy * NX + NX):
            if s:
                arrived(dq_in.at[s], dq_sem.at[s])
                dq += dq_in[s].astype(F32)
    out_ref[0] = (dq * FACTOR).astype(BF16)
    dk, dv = dk_acc[rows(0)], dv_acc[rows(0)]
    for p in (2, 3, 6, 7, 4, 5, 1):
        arrived(z_in.at[p], z_sem.at[p])
        dk += z_in[p, 0].astype(F32)
        dv += z_in[p, 1].astype(F32)
    out_ref[1] = (dk * FACTOR).astype(BF16)
    out_ref[2] = dv.astype(BF16)
    of(q_land.at[pl.ds(1, 15)], 0, q_sem.at[0]).wait_send()
    of(d_land.at[pl.ds(1, 15)], 1, q_sem.at[0]).wait_send()
    of(kv.at[:, pl.ds(0, 15 * TOK)], 2, q_sem.at[0]).wait_send()
    of(sib_out, 3, q_sem.at[0]).wait_send()
    of(z_out.at[pl.ds(1, 7)], 4, q_sem.at[0]).wait_send()
    of(dq_out.at[pl.ds(1, 15)], 5, q_sem.at[0]).wait_send()


def on_device(*args):
    vmem, dma = pltpu.VMEM, pltpu.SemaphoreType.DMA
    blocks = NX * NY
    out = pl.pallas_call(
        kernel,
        out_shape=jax.ShapeDtypeStruct((3, TOK, HEAD), BF16),
        in_specs=[pl.BlockSpec(memory_space=pltpu.HBM)] * 6,
        out_specs=pl.BlockSpec(memory_space=pltpu.VMEM),
        scratch_shapes=[
            vmem((blocks, TOK + AUX, HEAD), BF16),
            vmem((blocks, TOK + AUX, HEAD), BF16),
            vmem((2, SIDE, HEAD), BF16),
            vmem((TOK, HEAD), BF16),
            vmem((TOK,), BF16),
            vmem((SIDE, HEAD), BF16),
            vmem((SIDE, HEAD), BF16),
            vmem((HEAD, SIDE), BF16),
            vmem((1, SIDE), F32),
            vmem((1, SIDE), F32),
            vmem((HEAD, SIDE), F32),
            vmem((SIDE, HEAD), F32),
            vmem((SIDE, HEAD), F32),
            vmem((NZ, 2, TOK, HEAD), BF16),
            vmem((NZ, 2, TOK, HEAD), BF16),
            vmem((NZ, 2, TOK, HEAD), BF16),
            vmem((NZ, 2, TOK, HEAD), BF16),
            vmem((blocks, TOK, HEAD), BF16),
            vmem((blocks, TOK, HEAD), BF16),
            dma((6,)),
            dma((6,)),
            dma((10,)),
            dma((10,)),
            dma((NZ,)),
            dma((NZ,)),
            dma((NZ,)),
            dma((NZ,)),
            dma((blocks,)),
        ],
        compiler_params=pltpu.CompilerParams(
            collective_id=0, has_side_effects=True, vmem_limit_bytes=62 << 20
        ),
        name="attention_backward",
    )(*args)
    return out[0], out[1], out[2]


def solution(mesh):
    tokens = P("ctx", None)
    return jax.shard_map(
        on_device,
        mesh=mesh,
        in_specs=(tokens,) * 5 + (P("ctx"),),
        out_specs=(tokens,) * 3,
        check_vma=False,
    )
```

```python
import math

import jax
import jax.numpy as jnp
from jax import lax
from jax.experimental import pallas as pl
from jax.experimental.pallas import tpu as pltpu
from jax.sharding import PartitionSpec as P

HEAD = 128
TOK = 128
AUX = 16
NX, NY, NZ = 4, 4, 8
KEYS = NZ * TOK
HALF = NX * TOK
ROW = 2 * HALF
QUERIES = NY * ROW
PAIR = 2 * TOK
FACTOR = HEAD**-0.5
LOG2E = math.log2(math.e)
F32, BF16 = jnp.float32, jnp.bfloat16
MESH = pl.DeviceIdType.MESH

Z_ORDER = (0, 1, 2, 6, 4, 7, 3, 5)
AT = {d: p for p, d in enumerate(Z_ORDER)}
A, B, C, D = range(4)
NEAR = (1, 3, 2)
ROW_AT = (0, 3, 2, 1)


def dot(a, b):
    return jnp.dot(a, b, preferred_element_type=F32)


def dot_nt(a, b):
    return lax.dot_general(a, b, (((1,), (1,)), ((), ())), preferred_element_type=F32)


def rows(block):
    return pl.ds(block * TOK, TOK)


def kernel(
    q_ref, k_ref, v_ref, so_ref, do_ref, lse_ref, out_ref,
    d_land, kv, so_buf, lse_buf, q_all, d_all, kt, lse_all, delta_all,
    dq_acc, dk_acc, dv_acc, z_out, z_in, sib_out, sib_in, dq_out, dq_in,
    local_sem, send_sem, q_sem, d_sem, kv_sem, sib_sem, z_sem, dq_sem,
):
    me = lax.axis_index("ctx")
    core, x = lax.rem(me, 2), lax.rem(me // 2, NX)
    y, z = lax.rem(me // (2 * NX), NY), me // (2 * NX * NY)

    def device(core, x, y, z):
        return ((z * NY + y) * NX + x) * 2 + core

    def at_xy(dx, dy):
        return device(core, lax.rem(x + dx, NX), lax.rem(y + dy, NY), z)

    def at_z(dz):
        return device(core, x, y, lax.rem(z + dz, NZ))

    sibling = device(1 - core, x, y, z)

    barrier = pltpu.get_barrier_semaphore()
    partners = [sibling]
    partners += [at_xy(d, 0) for d in NEAR] + [at_xy(0, d) for d in NEAR]
    partners += [at_z(d) for d in (1, 7, 2, 6)]
    for p in partners:
        pl.semaphore_signal(barrier, 1, device_id=(p,), device_id_type=MESH)

    fetch = [
        pltpu.make_async_copy(src, dst, local_sem.at[i])
        for i, (src, dst) in enumerate((
            (q_ref, q_all.at[pl.ds(0, TOK)]),
            (lse_ref, lse_buf),
            (so_ref, so_buf),
            (do_ref, d_land.at[0, pl.ds(0, TOK)]),
            (k_ref, kv.at[0, rows(0)]),
            (v_ref, kv.at[1, rows(0)]),
        ))
    ]
    for copy in fetch:
        copy.start()
    pl.semaphore_wait(barrier, len(partners))

    def send(src, dst, kind, recv_sem, target):
        pltpu.make_async_remote_copy(
            src_ref=src, dst_ref=dst, send_sem=send_sem.at[kind], recv_sem=recv_sem,
            device_id=(target,), device_id_type=MESH,
        ).start()

    def of(ref, kind, recv_sem):
        return pltpu.make_async_remote_copy(
            src_ref=ref, dst_ref=ref, send_sem=send_sem.at[kind], recv_sem=recv_sem,
            device_id=(sibling,), device_id_type=MESH,
        )

    def arrived(dst, recv_sem):
        of(dst, 0, recv_sem).wait_recv()

    def kv_at(p):
        return kv.at[:, rows(p)]

    def send_kv(src, d, dz):
        send(src, kv_at(AT[d]), 2, kv_sem.at[AT[d]], at_z(dz))

    def queries(dx, dy, other=0, n=1):
        return q_all.at[pl.ds(ROW_AT[dy] * ROW + other * HALF + dx * TOK, n * TOK)]

    def send_q(src, dx, dy, sem, hx, hy):
        send(src, queries(dx, dy), 0, q_sem.at[sem], at_xy(hx, hy))

    def send_d(src, dx, dy, sem, hx, hy):
        send(d_land.at[src], d_land.at[dy * NX + dx], 1, d_sem.at[sem], at_xy(hx, hy))

    for d in (2, 6, 1, 7):
        for h, src in enumerate((k_ref, v_ref)):
            send(src, kv.at[h, rows(AT[d])], 2, kv_sem.at[AT[d]], at_z(d))
    for d in NEAR:
        send_q(q_ref, d, 0, d, d, 0)
    for i in (1, 2, 3):
        fetch[i].wait()
    product = d_land[0, pl.ds(0, TOK)].astype(F32) * so_buf[...].astype(F32)
    delta_row = jnp.sum(product.T, axis=0, keepdims=True)
    lse_row = jnp.reshape(lse_buf[...].astype(F32), (1, TOK))
    first = lax.broadcasted_iota(jnp.int32, (AUX, TOK), 0) == 0
    d_land[0, pl.ds(TOK, AUX)] = jnp.where(first, lse_row, delta_row).astype(BF16)
    for d in NEAR:
        send_d(0, 0, d, 3 + d, 0, d)
    for d in NEAR:
        send_d(0, d, 0, d, d, 0)
        send_q(q_ref, 0, d, 3 + d, 0, d)
    fetch[0].wait()
    fetch[4].wait()
    fetch[5].wait()
    dq_acc[...] = jnp.zeros_like(dq_acc)
    dk_acc[...] = jnp.zeros_like(dk_acc)
    dv_acc[...] = jnp.zeros_like(dv_acc)

    def row(dy, other):
        return pl.ds(other * NX * NY + dy * NX, NX)

    def take(dy, other):
        for s in range(NX):
            block = other * NX * NY + dy * NX + s
            to = pl.ds(ROW_AT[dy] * ROW + other * HALF + s * TOK, TOK)
            d_all[to] = d_land[block, pl.ds(0, TOK)]
            aux = d_land[block, pl.ds(TOK, AUX)].astype(F32)
            lse_all[:, to] = aux[0:1] * LOG2E
            delta_all[:, to] = aux[1:2]

    def land(dy):
        if dy:
            arrived(queries(0, dy), q_sem.at[3 + dy])
            arrived(queries(1, dy, 0, 3), q_sem.at[6 + dy])
            arrived(d_land.at[pl.ds(dy * NX + 1, 3)], d_sem.at[6 + dy])
        else:
            for e in NEAR:
                arrived(d_land.at[e], d_sem.at[e])
        send(queries(0, dy, 0, NX), queries(0, dy, 1, NX), 0, q_sem.at[10 + dy], sibling)
        send(d_land.at[row(dy, 0)], d_land.at[row(dy, 1)], 1, d_sem.at[10 + dy], sibling)
        take(dy, 0)

    def land_other(dy):
        arrived(queries(0, dy, 1, NX), q_sem.at[10 + dy])
        arrived(d_land.at[row(dy, 1)], d_sem.at[10 + dy])
        take(dy, 1)

    def keys_ready(g):
        for p in (2 * g, 2 * g + 1):
            if p:
                arrived(kv_at(p), kv_sem.at[p])
        ks = pl.ds(g * PAIR, PAIR)
        kt[:, ks] = kv[0, ks].T

    def tile(k0, kn, q0, qn):
        ks, qs = pl.ds(k0, kn), pl.ds(q0, qn)
        scores = dot_nt(kv[0, ks], q_all[qs])
        probs = dot_nt(kv[1, ks], d_all[qs])
        weights = jnp.exp2(scores * (FACTOR * LOG2E) - lse_all[:, qs])
        grads = (weights * (probs - delta_all[:, qs])).astype(BF16)
        dv_acc[ks] += dot(weights.astype(BF16), d_all[qs])
        dk_acc[ks] += dot(grads, q_all[qs])
        dq_acc[:, qs] += dot(kt[:, ks], grads)

    def near_tile(dy, other):
        tile(0, 2 * PAIR, ROW_AT[dy] * ROW + other * HALF, HALF)

    def far_tile(g, first, n):
        tile(g * PAIR, PAIR, first * ROW, n * ROW)

    def to_owner(g):
        for p in (2 * g, 2 * g + 1):
            if p:
                z_out[p, 0] = dk_acc[rows(p)].astype(BF16)
                z_out[p, 1] = dv_acc[rows(p)].astype(BF16)
                send(z_out.at[p], z_in.at[p], 3, z_sem.at[p], at_z(NZ - Z_ORDER[p]))

    def partial(dy, other, dx):
        return dq_acc[:, pl.ds(ROW_AT[dy] * ROW + other * HALF + dx * TOK, TOK)]

    def to_sibling(dy):
        for dx in range(NX):
            sib_out[dy * NX + dx] = partial(dy, 1, dx).astype(BF16)
        r = row(dy, 0)
        send(sib_out.at[r], sib_in.at[r], 4, sib_sem.at[dy], sibling)

    def queries_done(dy):
        r = row(dy, 0)
        arrived(sib_in.at[r], sib_sem.at[dy])
        for dx in (0, 1, 3, 2):
            s = dy * NX + dx
            if s:
                dq_out[s] = (partial(dy, 0, dx) + sib_in[s].astype(F32)).astype(BF16)
                send(dq_out.at[s], dq_in.at[s], 5, dq_sem.at[s], at_xy((NX - dx) % NX, (NY - dy) % NY))

    for e in NEAR:
        arrived(queries(e, 0), q_sem.at[e])
        for d in NEAR:
            send_q(queries(e, 0), e, d, 6 + d, 0, d)
        arrived(d_land.at[e * NX], d_sem.at[3 + e])
        for d in NEAR:
            send_d(e * NX, d, e, 6 + e, d, 0)
    land(0)
    for d, far, hop, mid, h in ((2, 3, 1, 2, 0), (6, 5, 7, 6, 1)):
        arrived(kv_at(AT[d]), kv_sem.at[AT[d]])
        send_kv(kv_at(AT[d]), far, hop)
        src, dst = kv.at[h, rows(AT[d])], kv.at[h, rows(AT[4])]
        send(src, dst, 2, kv_sem.at[AT[4]], at_z(mid))
    ks = pl.ds(B * PAIR, PAIR)
    kt[:, ks] = kv[0, ks].T
    tile(PAIR, PAIR, 0, HALF)
    keys_ready(A)
    tile(0, PAIR, 0, HALF)
    land_other(0)
    near_tile(0, 1)
    land(3)
    near_tile(3, 0)
    land(1)
    land(2)
    keys_ready(D)
    keys_ready(C)
    near_tile(2, 0)
    far_tile(D, 0, 1)
    far_tile(C, 0, 1)
    to_sibling(0)
    land_other(3)
    land_other(1)
    land_other(2)
    far_tile(D, 1, 3)
    to_owner(D)
    near_tile(2, 1)
    far_tile(C, 2, 1)
    far_tile(C, 1, 1)
    to_sibling(2)
    queries_done(0)
    far_tile(C, 3, 1)
    near_tile(3, 1)
    to_owner(C)
    to_sibling(3)
    queries_done(2)
    near_tile(1, 1)
    to_sibling(1)
    queries_done(3)
    near_tile(1, 0)
    to_owner(B)
    to_owner(A)
    queries_done(1)
    dq = partial(0, 0, 0) + sib_in[0].astype(F32)
    for dy in (0, 3, 2, 1):
        for s in range(dy * NX, dy * NX + NX):
            if s:
                arrived(dq_in.at[s], dq_sem.at[s])
                dq += dq_in[s].astype(F32)
    out_ref[0] = (dq.T * FACTOR).astype(BF16)
    dk, dv = dk_acc[rows(0)], dv_acc[rows(0)]
    for p in (6, 7, 4, 5, 1, 2, 3):
        arrived(z_in.at[p], z_sem.at[p])
        dk += z_in[p, 0].astype(F32)
        dv += z_in[p, 1].astype(F32)
    out_ref[1] = (dk * FACTOR).astype(BF16)
    out_ref[2] = dv.astype(BF16)
    of(q_all.at[pl.ds(0, 31 * TOK)], 0, q_sem.at[0]).wait_send()
    of(d_land.at[pl.ds(1, 31)], 1, q_sem.at[0]).wait_send()
    of(kv.at[:, pl.ds(0, 7 * TOK)], 2, q_sem.at[0]).wait_send()
    of(z_out.at[pl.ds(1, 7)], 3, q_sem.at[0]).wait_send()
    of(sib_out, 4, q_sem.at[0]).wait_send()
    of(dq_out.at[pl.ds(1, 15)], 5, q_sem.at[0]).wait_send()


def on_device(*args):
    vmem, dma = pltpu.VMEM, pltpu.SemaphoreType.DMA
    blocks = NX * NY
    out = pl.pallas_call(
        kernel,
        out_shape=jax.ShapeDtypeStruct((3, TOK, HEAD), BF16),
        in_specs=[pl.BlockSpec(memory_space=pltpu.HBM)] * 6,
        out_specs=pl.BlockSpec(memory_space=pltpu.VMEM),
        scratch_shapes=[
            vmem((2 * blocks, TOK + AUX, HEAD), BF16),
            vmem((2, KEYS, HEAD), BF16),
            vmem((TOK, HEAD), BF16),
            vmem((TOK,), BF16),
            vmem((QUERIES, HEAD), BF16),
            vmem((QUERIES, HEAD), BF16),
            vmem((HEAD, KEYS), BF16),
            vmem((1, QUERIES), F32),
            vmem((1, QUERIES), F32),
            vmem((HEAD, QUERIES), F32),
            vmem((KEYS, HEAD), F32),
            vmem((KEYS, HEAD), F32),
            vmem((NZ, 2, TOK, HEAD), BF16),
            vmem((NZ, 2, TOK, HEAD), BF16),
            vmem((blocks, HEAD, TOK), BF16),
            vmem((blocks, HEAD, TOK), BF16),
            vmem((blocks, HEAD, TOK), BF16),
            vmem((blocks, HEAD, TOK), BF16),
            dma((6,)),
            dma((6,)),
            dma((14,)),
            dma((14,)),
            dma((NZ,)),
            dma((NY,)),
            dma((NZ,)),
            dma((blocks,)),
        ],
        compiler_params=pltpu.CompilerParams(
            collective_id=0, has_side_effects=True, vmem_limit_bytes=62 << 20
        ),
        name="attention_backward",
    )(*args)
    return out[0], out[1], out[2]


def solution(mesh):
    tokens = P("ctx", None)
    return jax.shard_map(
        on_device,
        mesh=mesh,
        in_specs=(tokens,) * 5 + (P("ctx"),),
        out_specs=(tokens,) * 3,
        check_vma=False,
    )
```

```python
import math

import jax
import jax.numpy as jnp
from jax import lax
from jax.experimental import pallas as pl
from jax.experimental.pallas import tpu as pltpu
from jax.sharding import PartitionSpec as P

HEAD = 128
TOK = 128
AUX = 16
NX, NY, NZ = 4, 4, 8
KEYS = NZ * TOK
HALF = NX * TOK
ROW = 2 * HALF
QUERIES = NY * ROW
PAIR = 2 * TOK
FACTOR = HEAD**-0.5
LOG2E = math.log2(math.e)
F32, BF16 = jnp.float32, jnp.bfloat16
MESH = pl.DeviceIdType.MESH

Z_ORDER = (0, 1, 2, 6, 4, 7, 3, 5)
AT = {d: p for p, d in enumerate(Z_ORDER)}
A, B, C, D = range(4)
NEAR = (1, 3, 2)
HALF_AT = ((0, 4, 3, 2), (1, 7, 6, 5))


def dot(a, b):
    return jnp.dot(a, b, preferred_element_type=F32)


def dot_nt(a, b):
    return lax.dot_general(a, b, (((1,), (1,)), ((), ())), preferred_element_type=F32)


def rows(block):
    return pl.ds(block * TOK, TOK)


def kernel(
    q_ref, k_ref, v_ref, so_ref, do_ref, lse_ref, out_ref,
    d_land, kv, so_buf, lse_buf, q_all, d_all, kt, lse_all, delta_all,
    dq_acc, dk_acc, dv_acc, z_out, z_in, sib_out, sib_in, dq_out, dq_in,
    local_sem, send_sem, q_sem, d_sem, kv_sem, sib_sem, z_sem, dq_sem,
):
    me = lax.axis_index("ctx")
    core, x = lax.rem(me, 2), lax.rem(me // 2, NX)
    y, z = lax.rem(me // (2 * NX), NY), me // (2 * NX * NY)

    def device(core, x, y, z):
        return ((z * NY + y) * NX + x) * 2 + core

    def at_xy(dx, dy):
        return device(core, lax.rem(x + dx, NX), lax.rem(y + dy, NY), z)

    def at_z(dz):
        return device(core, x, y, lax.rem(z + dz, NZ))

    sibling = device(1 - core, x, y, z)

    barrier = pltpu.get_barrier_semaphore()
    partners = [sibling]
    partners += [at_xy(d, 0) for d in NEAR] + [at_xy(0, d) for d in NEAR]
    partners += [at_z(d) for d in (1, 7, 2, 6)]
    for p in partners:
        pl.semaphore_signal(barrier, 1, device_id=(p,), device_id_type=MESH)

    fetch = [
        pltpu.make_async_copy(src, dst, local_sem.at[i])
        for i, (src, dst) in enumerate((
            (q_ref, q_all.at[pl.ds(0, TOK)]),
            (lse_ref, lse_buf),
            (so_ref, so_buf),
            (do_ref, d_land.at[0, pl.ds(0, TOK)]),
            (k_ref, kv.at[0, rows(0)]),
            (v_ref, kv.at[1, rows(0)]),
        ))
    ]
    for copy in fetch:
        copy.start()
    pl.semaphore_wait(barrier, len(partners))

    def send(src, dst, kind, recv_sem, target):
        pltpu.make_async_remote_copy(
            src_ref=src, dst_ref=dst, send_sem=send_sem.at[kind], recv_sem=recv_sem,
            device_id=(target,), device_id_type=MESH,
        ).start()

    def of(ref, kind, recv_sem):
        return pltpu.make_async_remote_copy(
            src_ref=ref, dst_ref=ref, send_sem=send_sem.at[kind], recv_sem=recv_sem,
            device_id=(sibling,), device_id_type=MESH,
        )

    def arrived(dst, recv_sem):
        of(dst, 0, recv_sem).wait_recv()

    def kv_at(p):
        return kv.at[:, rows(p)]

    def kv_arrival(p):
        return kv_sem.at[p if p < 4 else p // 2 + 2]

    def send_kv(src, d, dz):
        send(src, kv_at(AT[d]), 2, kv_arrival(AT[d]), at_z(dz))

    def queries(dx, dy, other=0, n=1):
        return q_all.at[pl.ds(HALF_AT[other][dy] * HALF + dx * TOK, n * TOK)]

    def send_q(src, dx, dy, sem, hx, hy):
        send(src, queries(dx, dy), 0, q_sem.at[sem], at_xy(hx, hy))

    def send_d(src, dx, dy, sem, hx, hy):
        send(d_land.at[src], d_land.at[dy * NX + dx], 1, d_sem.at[sem], at_xy(hx, hy))

    for d in (2, 6, 1, 7):
        for h, src in enumerate((k_ref, v_ref)):
            send(src, kv.at[h, rows(AT[d])], 2, kv_arrival(AT[d]), at_z(d))
    for d in NEAR:
        send_q(q_ref, d, 0, d, d, 0)
    for i in (1, 2, 3):
        fetch[i].wait()
    product = d_land[0, pl.ds(0, TOK)].astype(F32) * so_buf[...].astype(F32)
    delta_row = jnp.sum(product.T, axis=0, keepdims=True)
    lse_row = jnp.reshape(lse_buf[...].astype(F32), (1, TOK))
    first = lax.broadcasted_iota(jnp.int32, (AUX, TOK), 0) == 0
    d_land[0, pl.ds(TOK, AUX)] = jnp.where(first, lse_row, delta_row).astype(BF16)
    for d in NEAR:
        send_d(0, 0, d, d, 0, d)
    for d in NEAR:
        send_d(0, d, 0, 4, d, 0)
        send_q(q_ref, 0, d, 3 + d, 0, d)
    fetch[0].wait()
    fetch[4].wait()
    fetch[5].wait()
    dq_acc[...] = jnp.zeros_like(dq_acc)
    dk_acc[...] = jnp.zeros_like(dk_acc)
    dv_acc[...] = jnp.zeros_like(dv_acc)

    def row(dy, other):
        return pl.ds(other * NX * NY + dy * NX, NX)

    def take(dy, other):
        for s in range(NX):
            block = other * NX * NY + dy * NX + s
            to = pl.ds(HALF_AT[other][dy] * HALF + s * TOK, TOK)
            d_all[to] = d_land[block, pl.ds(0, TOK)]
            aux = d_land[block, pl.ds(TOK, AUX)].astype(F32)
            lse_all[:, to] = aux[0:1] * LOG2E
            delta_all[:, to] = aux[1:2]

    def land(dy):
        if dy:
            arrived(queries(0, dy, 0, NX), q_sem.at[3 + dy])
            arrived(d_land.at[pl.ds(dy * NX + 1, 3)], d_sem.at[4 + dy])
        else:
            arrived(d_land.at[pl.ds(1, 3)], d_sem.at[4])
        sem = 7 if dy == 0 else 8
        send(queries(0, dy, 0, NX), queries(0, dy, 1, NX), 0, q_sem.at[sem], sibling)
        send(d_land.at[row(dy, 0)], d_land.at[row(dy, 1)], 1, d_sem.at[sem + 1], sibling)
        take(dy, 0)

    def land_other_0():
        arrived(queries(0, 0, 1, NX), q_sem.at[7])
        arrived(d_land.at[row(0, 1)], d_sem.at[8])
        take(0, 1)

    def land_other_rest():
        arrived(queries(0, 3, 1, 3 * NX), q_sem.at[8])
        arrived(d_land.at[pl.ds(NX * NY + NX, 3 * NX)], d_sem.at[9])
        for dy in (3, 2, 1):
            take(dy, 1)

    def keys_ready(g):
        ks = pl.ds(g * PAIR, PAIR)
        if g >= C:
            arrived(kv.at[:, ks], kv_sem.at[2 + g])
        else:
            arrived(kv_at(1), kv_sem.at[1])
        kt[:, ks] = kv[0, ks].T

    def tile(k0, kn, q0, qn):
        ks, qs = pl.ds(k0, kn), pl.ds(q0, qn)
        scores = dot_nt(kv[0, ks], q_all[qs])
        probs = dot_nt(kv[1, ks], d_all[qs])
        weights = jnp.exp2(scores * (FACTOR * LOG2E) - lse_all[:, qs])
        grads = (weights * (probs - delta_all[:, qs])).astype(BF16)
        dv_acc[ks] += dot(weights.astype(BF16), d_all[qs])
        dk_acc[ks] += dot(grads, q_all[qs])
        dq_acc[:, qs] += dot(kt[:, ks], grads)

    def near_tile(dy, other):
        tile(0, 2 * PAIR, HALF_AT[other][dy] * HALF, HALF)

    def far_tile(g, dy):
        if dy == 0:
            tile(g * PAIR, PAIR, 0, ROW)
        else:
            for other in range(2):
                tile(g * PAIR, PAIR, HALF_AT[other][dy] * HALF, HALF)

    def to_owner(g):
        for p in (2 * g, 2 * g + 1):
            if p:
                z_out[p, 0] = dk_acc[rows(p)].astype(BF16)
                z_out[p, 1] = dv_acc[rows(p)].astype(BF16)
                send(z_out.at[p], z_in.at[p], 3, z_sem.at[p // 4], at_z(NZ - Z_ORDER[p]))

    def partial(dy, other, dx):
        return dq_acc[:, pl.ds(HALF_AT[other][dy] * HALF + dx * TOK, TOK)]

    def to_sibling(dy):
        for dx in range(NX):
            sib_out[dy * NX + dx] = partial(dy, 1, dx).astype(BF16)
        r = row(dy, 0)
        send(sib_out.at[r], sib_in.at[r], 4, sib_sem.at[dy], sibling)

    def queries_done(dy):
        r = row(dy, 0)
        arrived(sib_in.at[r], sib_sem.at[dy])
        for dx in (0, 1, 3, 2):
            s = dy * NX + dx
            if s:
                dq_out[s] = (partial(dy, 0, dx) + sib_in[s].astype(F32)).astype(BF16)
                send(dq_out.at[s], dq_in.at[s], 5, dq_sem.at[min(dy, 2)], at_xy((NX - dx) % NX, (NY - dy) % NY))

    for e in NEAR:
        arrived(queries(e, 0), q_sem.at[e])
        for d in NEAR:
            send_q(queries(e, 0), e, d, 3 + d, 0, d)
        arrived(d_land.at[e * NX], d_sem.at[e])
        for d in NEAR:
            send_d(e * NX, d, e, 4 + e, d, 0)
    land(0)
    for d, far, hop, mid, h in ((2, 3, 1, 2, 0), (6, 5, 7, 6, 1)):
        arrived(kv_at(AT[d]), kv_sem.at[AT[d]])
        send_kv(kv_at(AT[d]), far, hop)
        src, dst = kv.at[h, rows(AT[d])], kv.at[h, rows(AT[4])]
        send(src, dst, 2, kv_arrival(AT[4]), at_z(mid))
    ks = pl.ds(B * PAIR, PAIR)
    kt[:, ks] = kv[0, ks].T
    tile(PAIR, PAIR, 0, HALF)
    keys_ready(A)
    tile(0, PAIR, 0, HALF)
    land_other_0()
    near_tile(0, 1)
    land(3)
    land(1)
    land(2)
    keys_ready(D)
    near_tile(3, 0)
    near_tile(2, 0)
    far_tile(D, 0)
    tile(D * PAIR, PAIR, 2 * HALF, 3 * HALF)
    land_other_rest()
    keys_ready(C)
    tile(D * PAIR, PAIR, 5 * HALF, 3 * HALF)
    to_owner(D)
    near_tile(2, 1)
    far_tile(C, 2)
    to_sibling(2)
    far_tile(C, 3)
    far_tile(C, 1)
    far_tile(C, 0)
    to_owner(C)
    to_sibling(0)
    queries_done(2)
    near_tile(3, 1)
    near_tile(1, 1)
    to_sibling(3)
    to_sibling(1)
    queries_done(0)
    near_tile(1, 0)
    to_owner(B)
    to_owner(A)
    queries_done(3)
    queries_done(1)
    dq = partial(0, 0, 0) + sib_in[0].astype(F32)
    for sem, first, n in ((0, 1, 3), (2, 8, 8), (1, 4, 4)):
        arrived(dq_in.at[pl.ds(first, n)], dq_sem.at[sem])
        for s in range(first, first + n):
            dq += dq_in[s].astype(F32)
    out_ref[0] = (dq.T * FACTOR).astype(BF16)
    dk, dv = dk_acc[rows(0)], dv_acc[rows(0)]
    for sem, first, n in ((1, 4, 4), (0, 1, 3)):
        arrived(z_in.at[pl.ds(first, n)], z_sem.at[sem])
        for p in range(first, first + n):
            dk += z_in[p, 0].astype(F32)
            dv += z_in[p, 1].astype(F32)
    out_ref[1] = (dk * FACTOR).astype(BF16)
    out_ref[2] = dv.astype(BF16)
    of(q_all.at[pl.ds(0, 31 * TOK)], 0, q_sem.at[0]).wait_send()
    of(d_land.at[pl.ds(1, 31)], 1, q_sem.at[0]).wait_send()
    of(kv.at[:, pl.ds(0, 7 * TOK)], 2, q_sem.at[0]).wait_send()
    of(z_out.at[pl.ds(1, 7)], 3, q_sem.at[0]).wait_send()
    of(sib_out, 4, q_sem.at[0]).wait_send()
    of(dq_out.at[pl.ds(1, 15)], 5, q_sem.at[0]).wait_send()


def on_device(*args):
    vmem, dma = pltpu.VMEM, pltpu.SemaphoreType.DMA
    blocks = NX * NY
    out = pl.pallas_call(
        kernel,
        out_shape=jax.ShapeDtypeStruct((3, TOK, HEAD), BF16),
        in_specs=[pl.BlockSpec(memory_space=pltpu.HBM)] * 6,
        out_specs=pl.BlockSpec(memory_space=pltpu.VMEM),
        scratch_shapes=[
            vmem((2 * blocks, TOK + AUX, HEAD), BF16),
            vmem((2, KEYS, HEAD), BF16),
            vmem((TOK, HEAD), BF16),
            vmem((TOK,), BF16),
            vmem((QUERIES, HEAD), BF16),
            vmem((QUERIES, HEAD), BF16),
            vmem((HEAD, KEYS), BF16),
            vmem((1, QUERIES), F32),
            vmem((1, QUERIES), F32),
            vmem((HEAD, QUERIES), F32),
            vmem((KEYS, HEAD), F32),
            vmem((KEYS, HEAD), F32),
            vmem((NZ, 2, TOK, HEAD), BF16),
            vmem((NZ, 2, TOK, HEAD), BF16),
            vmem((blocks, HEAD, TOK), BF16),
            vmem((blocks, HEAD, TOK), BF16),
            vmem((blocks, HEAD, TOK), BF16),
            vmem((blocks, HEAD, TOK), BF16),
            dma((6,)),
            dma((6,)),
            dma((9,)),
            dma((10,)),
            dma((6,)),
            dma((NY,)),
            dma((2,)),
            dma((3,)),
        ],
        compiler_params=pltpu.CompilerParams(
            collective_id=0, has_side_effects=True, vmem_limit_bytes=62 << 20
        ),
        name="attention_backward",
    )(*args)
    return out[0], out[1], out[2]


def solution(mesh):
    tokens = P("ctx", None)
    return jax.shard_map(
        on_device,
        mesh=mesh,
        in_specs=(tokens,) * 5 + (P("ctx"),),
        out_specs=(tokens,) * 3,
        check_vma=False,
    )
```

```python
import math

import jax
import jax.numpy as jnp
from jax import lax
from jax.experimental import pallas as pl
from jax.experimental.pallas import tpu as pltpu
from jax.sharding import PartitionSpec as P

HEAD = 128
TOK = 128
AUX = 16
NX, NY, NZ = 4, 4, 8
KEYS = NZ * TOK
HALF = NX * TOK
ROW = 2 * HALF
QUERIES = NY * ROW
PAIR = 2 * TOK
FACTOR = HEAD**-0.5
LOG2E = math.log2(math.e)
F32, BF16 = jnp.float32, jnp.bfloat16
MESH = pl.DeviceIdType.MESH

Z_ORDER = (0, 1, 2, 6, 4, 7, 3, 5)
AT = {d: p for p, d in enumerate(Z_ORDER)}
A, B, C, D = range(4)
NEAR = (1, 3, 2)
HALF_AT = ((0, 4, 3, 2), (1, 7, 6, 5))


def dot(a, b):
    return jnp.dot(a, b, preferred_element_type=F32)


def dot_nt(a, b):
    return lax.dot_general(a, b, (((1,), (1,)), ((), ())), preferred_element_type=F32)


def rows(block):
    return pl.ds(block * TOK, TOK)


def kernel(
    q_ref, k_ref, v_ref, so_ref, do_ref, lse_ref, out_ref,
    d_land, kv, so_buf, lse_buf, q_all, d_all, kt, lse_all, delta_all,
    dq_acc, dk_acc, dv_acc, z_out, z_in, sib_out, sib_in, dq_out, dq_in, out_buf,
    local_sem, send_sem, q_sem, d_sem, kv_sem, sib_sem, z_sem, dq_sem,
):
    me = lax.axis_index("ctx")
    core, x = lax.rem(me, 2), lax.rem(me // 2, NX)
    y, z = lax.rem(me // (2 * NX), NY), me // (2 * NX * NY)

    def device(core, x, y, z):
        return ((z * NY + y) * NX + x) * 2 + core

    def at_xy(dx, dy):
        return device(core, lax.rem(x + dx, NX), lax.rem(y + dy, NY), z)

    def at_z(dz):
        return device(core, x, y, lax.rem(z + dz, NZ))

    sibling = device(1 - core, x, y, z)

    barrier = pltpu.get_barrier_semaphore()
    partners = [sibling]
    partners += [at_xy(d, 0) for d in NEAR] + [at_xy(0, d) for d in NEAR]
    partners += [at_z(d) for d in (1, 7, 2, 6)]
    for p in partners:
        pl.semaphore_signal(barrier, 1, device_id=(p,), device_id_type=MESH)

    fetch = [
        pltpu.make_async_copy(src, dst, local_sem.at[i])
        for i, (src, dst) in enumerate((
            (q_ref, q_all.at[pl.ds(0, TOK)]),
            (lse_ref, lse_buf),
            (so_ref, so_buf),
            (do_ref, d_land.at[0, pl.ds(0, TOK)]),
            (k_ref, kv.at[0, rows(0)]),
            (v_ref, kv.at[1, rows(0)]),
        ))
    ]
    for copy in fetch:
        copy.start()
    pl.semaphore_wait(barrier, len(partners))

    def send(src, dst, kind, recv_sem, target):
        pltpu.make_async_remote_copy(
            src_ref=src, dst_ref=dst, send_sem=send_sem.at[kind], recv_sem=recv_sem,
            device_id=(target,), device_id_type=MESH,
        ).start()

    def of(ref, kind, recv_sem):
        return pltpu.make_async_remote_copy(
            src_ref=ref, dst_ref=ref, send_sem=send_sem.at[kind], recv_sem=recv_sem,
            device_id=(sibling,), device_id_type=MESH,
        )

    def arrived(dst, recv_sem):
        of(dst, 0, recv_sem).wait_recv()

    def kv_at(p):
        return kv.at[:, rows(p)]

    def kv_arrival(p):
        return kv_sem.at[p if p < 4 else p // 2 + 2]

    def send_kv(src, d, dz):
        send(src, kv_at(AT[d]), 2, kv_arrival(AT[d]), at_z(dz))

    def queries(dx, dy, other=0, n=1):
        return q_all.at[pl.ds(HALF_AT[other][dy] * HALF + dx * TOK, n * TOK)]

    def send_q(src, dx, dy, sem, hx, hy):
        send(src, queries(dx, dy), 0, q_sem.at[sem], at_xy(hx, hy))

    def send_d(src, dx, dy, sem, hx, hy):
        send(d_land.at[src], d_land.at[dy * NX + dx], 1, d_sem.at[sem], at_xy(hx, hy))

    for d in (2, 6, 1, 7):
        for h, src in enumerate((k_ref, v_ref)):
            send(src, kv.at[h, rows(AT[d])], 2, kv_arrival(AT[d]), at_z(d))
    for d in NEAR:
        send_q(q_ref, d, 0, d, d, 0)
    for i in (1, 2, 3):
        fetch[i].wait()
    product = d_land[0, pl.ds(0, TOK)].astype(F32) * so_buf[...].astype(F32)
    delta_row = jnp.sum(product.T, axis=0, keepdims=True)
    lse_row = jnp.reshape(lse_buf[...].astype(F32), (1, TOK))
    first = lax.broadcasted_iota(jnp.int32, (AUX, TOK), 0) == 0
    d_land[0, pl.ds(TOK, AUX)] = jnp.where(first, lse_row, delta_row).astype(BF16)
    for d in NEAR:
        send_d(0, 0, d, d, 0, d)
    for d in NEAR:
        send_d(0, d, 0, 4, d, 0)
        send_q(q_ref, 0, d, 3 + d, 0, d)
    fetch[0].wait()
    fetch[4].wait()
    fetch[5].wait()
    dq_acc[...] = jnp.zeros_like(dq_acc)
    dk_acc[...] = jnp.zeros_like(dk_acc)
    dv_acc[...] = jnp.zeros_like(dv_acc)

    def row(dy, other):
        return pl.ds(other * NX * NY + dy * NX, NX)

    def take(dy, other):
        for s in range(NX):
            block = other * NX * NY + dy * NX + s
            to = pl.ds(HALF_AT[other][dy] * HALF + s * TOK, TOK)
            d_all[to] = d_land[block, pl.ds(0, TOK)]
            aux = d_land[block, pl.ds(TOK, AUX)].astype(F32)
            lse_all[:, to] = aux[0:1] * LOG2E
            delta_all[:, to] = aux[1:2]

    def land(dy):
        if dy:
            arrived(queries(0, dy, 0, NX), q_sem.at[3 + dy])
            arrived(d_land.at[pl.ds(dy * NX + 1, 3)], d_sem.at[4 + dy])
        else:
            arrived(d_land.at[pl.ds(1, 3)], d_sem.at[4])
        sem = 7 if dy == 0 else 8
        send(queries(0, dy, 0, NX), queries(0, dy, 1, NX), 0, q_sem.at[sem], sibling)
        send(d_land.at[row(dy, 0)], d_land.at[row(dy, 1)], 1, d_sem.at[sem + 1], sibling)
        take(dy, 0)

    def land_other_0():
        arrived(queries(0, 0, 1, NX), q_sem.at[7])
        arrived(d_land.at[row(0, 1)], d_sem.at[8])
        take(0, 1)

    def land_other_rest():
        arrived(queries(0, 3, 1, 3 * NX), q_sem.at[8])
        arrived(d_land.at[pl.ds(NX * NY + NX, 3 * NX)], d_sem.at[9])
        for dy in (3, 2, 1):
            take(dy, 1)

    def keys_ready(g):
        ks = pl.ds(g * PAIR, PAIR)
        if g >= C:
            arrived(kv.at[:, ks], kv_sem.at[2 + g])
        else:
            arrived(kv_at(1), kv_sem.at[1])
        kt[:, ks] = kv[0, ks].T

    def tile(k0, kn, q0, qn):
        ks, qs = pl.ds(k0, kn), pl.ds(q0, qn)
        scores = dot_nt(kv[0, ks], q_all[qs])
        probs = dot_nt(kv[1, ks], d_all[qs])
        weights = jnp.exp2(scores * (FACTOR * LOG2E) - lse_all[:, qs])
        grads = (weights * (probs - delta_all[:, qs])).astype(BF16)
        dv_acc[ks] += dot(weights.astype(BF16), d_all[qs])
        dk_acc[ks] += dot(grads, q_all[qs])
        dq_acc[:, qs] += dot(kt[:, ks], grads)

    def near_tile(dy, other):
        tile(0, 2 * PAIR, HALF_AT[other][dy] * HALF, HALF)

    def far_tile(g, dy):
        if dy == 0:
            tile(g * PAIR, PAIR, 0, ROW)
        else:
            for other in range(2):
                tile(g * PAIR, PAIR, HALF_AT[other][dy] * HALF, HALF)

    def to_owner(g):
        for p in (2 * g, 2 * g + 1):
            if p:
                z_out[p, 0] = dk_acc[rows(p)].astype(BF16)
                z_out[p, 1] = dv_acc[rows(p)].astype(BF16)
                send(z_out.at[p], z_in.at[p], 3, z_sem.at[p // 4], at_z(NZ - Z_ORDER[p]))

    def partial(dy, other, dx):
        return dq_acc[:, pl.ds(HALF_AT[other][dy] * HALF + dx * TOK, TOK)]

    def to_sibling(dy):
        for dx in range(NX):
            sib_out[dy * NX + dx] = partial(dy, 1, dx).astype(BF16)
        r = row(dy, 0)
        send(sib_out.at[r], sib_in.at[r], 4, sib_sem.at[dy], sibling)

    def queries_done(dy):
        r = row(dy, 0)
        arrived(sib_in.at[r], sib_sem.at[dy])
        for dx in (0, 1, 3, 2):
            s = dy * NX + dx
            if s:
                dq_out[s] = (partial(dy, 0, dx) + sib_in[s].astype(F32)).astype(BF16)
                send(dq_out.at[s], dq_in.at[s], 5, dq_sem.at[min(dy, 2)], at_xy((NX - dx) % NX, (NY - dy) % NY))

    for e in NEAR:
        arrived(queries(e, 0), q_sem.at[e])
        for d in NEAR:
            send_q(queries(e, 0), e, d, 3 + d, 0, d)
        arrived(d_land.at[e * NX], d_sem.at[e])
        for d in NEAR:
            send_d(e * NX, d, e, 4 + e, d, 0)
    land(0)
    for d, far, hop, mid, h in ((2, 3, 1, 2, 0), (6, 5, 7, 6, 1)):
        arrived(kv_at(AT[d]), kv_sem.at[AT[d]])
        send_kv(kv_at(AT[d]), far, hop)
        src, dst = kv.at[h, rows(AT[d])], kv.at[h, rows(AT[4])]
        send(src, dst, 2, kv_arrival(AT[4]), at_z(mid))
    ks = pl.ds(B * PAIR, PAIR)
    kt[:, ks] = kv[0, ks].T
    tile(PAIR, PAIR, 0, HALF)
    keys_ready(A)
    tile(0, PAIR, 0, HALF)
    land_other_0()
    near_tile(0, 1)
    land(3)
    land(1)
    land(2)
    keys_ready(D)
    near_tile(3, 0)
    near_tile(2, 0)
    far_tile(D, 0)
    tile(D * PAIR, PAIR, 2 * HALF, 3 * HALF)
    land_other_rest()
    keys_ready(C)
    tile(D * PAIR, PAIR, 5 * HALF, 3 * HALF)
    to_owner(D)
    near_tile(2, 1)
    far_tile(C, 2)
    to_sibling(2)
    far_tile(C, 3)
    far_tile(C, 1)
    far_tile(C, 0)
    to_owner(C)
    to_sibling(0)
    queries_done(2)
    near_tile(3, 1)
    near_tile(1, 1)
    to_sibling(3)
    to_sibling(1)
    queries_done(0)
    near_tile(1, 0)
    to_owner(B)
    to_owner(A)
    queries_done(3)
    queries_done(1)
    def add_keys(dk, dv, sem, first, n):
        arrived(z_in.at[pl.ds(first, n)], z_sem.at[sem])
        for p in range(first, first + n):
            dk += z_in[p, 0].astype(F32)
            dv += z_in[p, 1].astype(F32)
        return dk, dv

    dk, dv = add_keys(dk_acc[rows(0)], dv_acc[rows(0)], 1, 4, 4)
    dq = partial(0, 0, 0) + sib_in[0].astype(F32)
    for sem, first, n in ((0, 1, 3), (2, 8, 8), (1, 4, 4)):
        arrived(dq_in.at[pl.ds(first, n)], dq_sem.at[sem])
        for s in range(first, first + n):
            dq += dq_in[s].astype(F32)
    out_buf[0] = (dq.T * FACTOR).astype(BF16)
    write_queries = pltpu.make_async_copy(out_buf.at[0], out_ref.at[0], local_sem.at[0])
    write_queries.start()
    dk, dv = add_keys(dk, dv, 0, 1, 3)
    out_buf[1] = (dk * FACTOR).astype(BF16)
    out_buf[2] = dv.astype(BF16)
    write_keys = pltpu.make_async_copy(out_buf.at[pl.ds(1, 2)], out_ref.at[pl.ds(1, 2)], local_sem.at[1])
    write_keys.start()
    of(q_all.at[pl.ds(0, 31 * TOK)], 0, q_sem.at[0]).wait_send()
    of(d_land.at[pl.ds(1, 31)], 1, q_sem.at[0]).wait_send()
    of(kv.at[:, pl.ds(0, 7 * TOK)], 2, q_sem.at[0]).wait_send()
    of(z_out.at[pl.ds(1, 7)], 3, q_sem.at[0]).wait_send()
    of(sib_out, 4, q_sem.at[0]).wait_send()
    of(dq_out.at[pl.ds(1, 15)], 5, q_sem.at[0]).wait_send()
    write_queries.wait()
    write_keys.wait()


def on_device(*args):
    vmem, dma = pltpu.VMEM, pltpu.SemaphoreType.DMA
    blocks = NX * NY
    out = pl.pallas_call(
        kernel,
        out_shape=jax.ShapeDtypeStruct((3, TOK, HEAD), BF16),
        in_specs=[pl.BlockSpec(memory_space=pltpu.HBM)] * 6,
        out_specs=pl.BlockSpec(memory_space=pltpu.HBM),
        scratch_shapes=[
            vmem((2 * blocks, TOK + AUX, HEAD), BF16),
            vmem((2, KEYS, HEAD), BF16),
            vmem((TOK, HEAD), BF16),
            vmem((TOK,), BF16),
            vmem((QUERIES, HEAD), BF16),
            vmem((QUERIES, HEAD), BF16),
            vmem((HEAD, KEYS), BF16),
            vmem((1, QUERIES), F32),
            vmem((1, QUERIES), F32),
            vmem((HEAD, QUERIES), F32),
            vmem((KEYS, HEAD), F32),
            vmem((KEYS, HEAD), F32),
            vmem((NZ, 2, TOK, HEAD), BF16),
            vmem((NZ, 2, TOK, HEAD), BF16),
            vmem((blocks, HEAD, TOK), BF16),
            vmem((blocks, HEAD, TOK), BF16),
            vmem((blocks, HEAD, TOK), BF16),
            vmem((blocks, HEAD, TOK), BF16),
            vmem((3, TOK, HEAD), BF16),
            dma((6,)),
            dma((6,)),
            dma((9,)),
            dma((10,)),
            dma((6,)),
            dma((NY,)),
            dma((2,)),
            dma((3,)),
        ],
        compiler_params=pltpu.CompilerParams(
            collective_id=0, has_side_effects=True, vmem_limit_bytes=62 << 20
        ),
        name="attention_backward",
    )(*args)
    return out[0], out[1], out[2]


def solution(mesh):
    tokens = P("ctx", None)
    return jax.shard_map(
        on_device,
        mesh=mesh,
        in_specs=(tokens,) * 5 + (P("ctx"),),
        out_specs=(tokens,) * 3,
        check_vma=False,
    )
```
